128 devices in a mesh: chan: 4 (over x), tile: 32 (over y, z, core).
Axes of the slice: x: 4, y: 4, z: 4, core: 2. Of those that a mesh axis runs over, the one named last changes fastest.
Arguments:
- voltages: bfloat16 [2, 128, 2048, 512], P(None, None, ('chan', 'tile')), may hold values from -6 to 6
- tile_pairs: int32 [528, 2], replicated, may hold values from 0 to 31, as said below
Outputs:
- visibilities: float32 [528, 128, 64, 128], P(None, ('chan', 'tile'))
The draws below stay inside these ranges and needn't reach their ends.
Inputs may be any that keep to these rules, and one draw needn't show every extreme that they name: `tile_pairs`: every pair of panels (p, q) with p <= q occurs in exactly one row; in every row the first entry is at most the second.
All inputs are finite; a program needn't handle non-finite values.
Results may differ from the reference program's by a relative error of at most 0.0003.
Values may be sent and summed in bfloat16 or wider, within the bound.
No kernel may reach another device: no remote copies, remote signals or barrier semaphores. Data moves between devices by JAX's collectives and lax.ppermute only.
A program may use at most 320 MiB of HBM per device.

```python
import jax
import jax.numpy as jnp
import numpy as np
from jax import lax

INPUTS = 2048
PANELS = 32
SPECTRA = 512
CHANS = 128
PANEL = 64


def draw_tile_pairs(key, part):
    listed = np.array([[row, col] for row in range(PANELS) for col in range(row, PANELS)], dtype=np.int32)
    order = jax.random.permutation(jax.random.fold_in(key, 11), listed.shape[0])
    return jnp.asarray(listed)[order]


def level_of(key, extent, split, smallest, top_value):
    gain = 1.0
    for position, blocks in split:
        heights = jax.random.uniform(jax.random.fold_in(jax.random.fold_in(key, 6), position), (blocks,), jnp.float32, smallest / len(split), top_value / len(split))
        gain = gain * jnp.repeat(jnp.exp(heights), extent[position] // blocks).reshape((-1,) + (1,) * (len(extent) - 1 - position))
    return gain


def gaussian(stream_key, dims, width, most, cuts=(), kind=jnp.bfloat16):
    gain = level_of(stream_key, dims, cuts, -0.22, 0.18) if cuts else 1.0
    entries = jax.random.normal(stream_key, dims, jnp.float32) * width * gain
    return jnp.minimum(jnp.maximum(entries, -most), most).astype(kind)


def setup_inputs(seed: int = 0) -> dict:
    key_list = jax.random.split(jax.random.key(seed), 3)
    return {
        "voltages": gaussian(key_list[0], (2, CHANS, INPUTS, SPECTRA), 1.0, 6.0, ((2, 128),)),
        "tile_pairs": draw_tile_pairs(jax.random.fold_in(key_list[2], 71), 0),
    }


def reference(voltages, tile_pairs):
    arranged = voltages.reshape(2, CHANS, PANELS, PANEL, SPECTRA)

    def one_slot(pair):
        row_data = lax.dynamic_index_in_dim(arranged, pair[0].astype(jnp.int32), 2, keepdims=False).astype(jnp.float32)
        col_data = lax.dynamic_index_in_dim(arranged, pair[1].astype(jnp.int32), 2, keepdims=False).astype(jnp.float32)
        hp = lax.Precision.HIGHEST
        real_part = jnp.einsum("fmt,fnt->fmn", row_data[0], col_data[0], precision=hp) + jnp.einsum("fmt,fnt->fmn", row_data[1], col_data[1], precision=hp)
        imag_part = jnp.einsum("fmt,fnt->fmn", row_data[1], col_data[0], precision=hp) - jnp.einsum("fmt,fnt->fmn", row_data[0], col_data[1], precision=hp)
        return jnp.concatenate((real_part, imag_part), axis=-1)

    result = lax.map(one_slot, tile_pairs)
    return result * (SPECTRA ** -0.5)
```

```python
import jax
import jax.numpy as jnp
from jax import lax
from jax.experimental import pallas as pl
from jax.experimental.pallas import tpu as pltpu
from jax.sharding import PartitionSpec as P

AXES = ("chan", "tile")
PANEL = 64
GROUP = 4


def visibilities(slot_ref, x_ref, out_ref, stacked, staged, sem, *, panels, scale):
    devices_per_panel = PANEL // x_ref.shape[2]
    spectra = x_ref.shape[3]
    blocks = panels // GROUP
    rows = GROUP * PANEL

    @pl.loop(0, panels)
    def _(p):
        here = pl.ds(p * devices_per_panel, devices_per_panel)
        real = x_ref[here, 0].reshape(PANEL, spectra)
        imag = x_ref[here, 1].reshape(PANEL, spectra)
        stacked[p, :PANEL, :spectra] = real
        stacked[p, :PANEL, spectra:] = imag
        stacked[p, PANEL:, :spectra] = -imag
        stacked[p, PANEL:, spectra:] = real

    def out_copy(place, i, j, a, b):
        slot = slot_ref[(i * GROUP + a) * panels + j * GROUP + b]
        return pltpu.make_async_copy(staged.at[place, a, b], out_ref.at[slot, 0], sem)

    @pl.loop(0, blocks)
    def _(j):
        right = stacked[pl.ds(j * GROUP, GROUP)].reshape(2 * rows, 2 * spectra)

        def pair(i):
            place = j * (j + 1) // 2 + i
            left = stacked[pl.ds(i * GROUP, GROUP), :PANEL].reshape(rows, 2 * spectra)
            product = lax.dot_general(
                left, right, (((1,), (1,)), ((), ())), preferred_element_type=jnp.float32
            )
            product = product * scale
            for a in range(GROUP):
                for b in range(GROUP):
                    staged[place, a, b] = product[
                        a * PANEL : (a + 1) * PANEL, b * 2 * PANEL : (b + 1) * 2 * PANEL
                    ]
            return place

        @pl.loop(0, j)
        def _(i):
            place = pair(i)
            for a in range(GROUP):
                for b in range(GROUP):
                    out_copy(place, i, j, a, b).start()

        place = pair(j)
        for a in range(GROUP):
            for b in range(a, GROUP):
                out_copy(place, j, j, a, b).start()

    pltpu.make_async_copy(out_ref, out_ref, sem).wait()


def body(voltages, tile_pairs):
    parts, chans, inputs_here, spectra = voltages.shape
    devices = lax.axis_size("chan") * lax.axis_size("tile")
    slots = tile_pairs.shape[0]
    panels = devices * inputs_here // PANEL
    blocks = panels // GROUP

    place = tile_pairs[:, 0] * panels + tile_pairs[:, 1]
    found = place[None, :] == jnp.arange(panels * panels, dtype=jnp.int32)[:, None]
    slot_of = jnp.sum(
        jnp.where(found, jnp.arange(slots, dtype=jnp.int32)[None, :], 0), axis=1
    )

    turned = lax.all_to_all(
        voltages.transpose(1, 0, 2, 3), AXES, split_axis=0, concat_axis=0, tiled=True
    )
    return pl.pallas_call(
        lambda *refs: visibilities(*refs, panels=panels, scale=spectra**-0.5),
        out_shape=jax.ShapeDtypeStruct((slots, 1, PANEL, 2 * PANEL), jnp.float32),
        in_specs=[
            pl.BlockSpec(memory_space=pltpu.SMEM),
            pl.BlockSpec(memory_space=pltpu.VMEM),
        ],
        out_specs=pl.BlockSpec(memory_space=pl.ANY),
        scratch_shapes=[
            pltpu.VMEM((panels, 2 * PANEL, 2 * spectra), jnp.bfloat16),
            pltpu.VMEM((blocks * (blocks + 1) // 2, GROUP, GROUP, PANEL, 2 * PANEL), jnp.float32),
            pltpu.SemaphoreType.DMA,
        ],
        compiler_params=pltpu.CompilerParams(vmem_limit_bytes=48 * 2**20),
        cost_estimate=pl.CostEstimate(
            flops=2 * slots * PANEL * 2 * PANEL * 2 * spectra,
            bytes_accessed=slots * PANEL * 2 * PANEL * 4,
            transcendentals=0,
        ),
        name="visibilities",
    )(slot_of, turned)


def solution(mesh):
    placed = (P(None, None, AXES, None), P())
    return jax.shard_map(
        body,
        mesh=mesh,
        in_specs=placed,
        out_specs=P(None, AXES, None, None),
        check_vma=False,
    )
```

```python
import jax
import jax.numpy as jnp
from jax import lax
from jax.experimental import pallas as pl
from jax.experimental.pallas import tpu as pltpu
from jax.sharding import PartitionSpec as P

AXES = ("chan", "tile")
PANEL = 64
LANES = 128
GROUP = 4
DEEP = 256
UNITS = 2


def by_channel(x_ref, y_ref, sem):
    parts, _, _, spectra = x_ref.shape
    for c in range(parts):
        for k in range(spectra // LANES):
            pltpu.make_async_copy(
                x_ref.at[c, :, :, pl.ds(k * LANES, LANES)], y_ref.at[:, c, k], sem
            ).start()
    pltpu.make_async_copy(y_ref, y_ref, sem).wait()


def visibilities(slot_ref, x_ref, out_ref, staged, sem, *, panels, scale):
    per_panel = PANEL // x_ref.shape[3]
    deep_per_part = x_ref.shape[2] * LANES // DEEP
    deeps = 2 * deep_per_part
    wide = DEEP // (2 * PANEL)

    def samples(first, last, part, deep):
        halves = [
            x_ref[first * per_panel : last * per_panel, part, deep * DEEP // LANES + h]
            .reshape((last - first) * PANEL, LANES)
            for h in range(DEEP // LANES)
        ]
        return jnp.concatenate(halves, axis=1)

    def left(first, deep):
        return samples(first, first + GROUP, deep // deep_per_part, deep % deep_per_part)

    def right(first, deep):
        part, deep = deep // deep_per_part, deep % deep_per_part
        rows = []
        for q in range(first, first + wide):
            if part == 0:
                rows += [samples(q, q + 1, 0, deep), -samples(q, q + 1, 1, deep)]
            else:
                rows += [samples(q, q + 1, 1, deep), samples(q, q + 1, 0, deep)]
        return jnp.concatenate(rows, axis=0)

    steps = [
        (i, j) for j in range(panels // GROUP) for i in range(j + 1)
    ]

    def run(*sums):
        def start(tiles):
            for place, p, q in tiles:
                pltpu.make_async_copy(
                    staged.at[place], out_ref.at[slot_ref[p * panels + q], 0], sem
                ).start()

        def drain(step):
            i, j = steps[step]
            tiles = []
            for unit in range(UNITS):
                product = pltpu.matmul_pop(sums[2 * unit + step % 2]) * scale
                for a in range(GROUP):
                    for b in range(wide):
                        p, q = i * GROUP + a, j * GROUP + unit * wide + b
                        place = (step * GROUP + a) * GROUP + unit * wide + b
                        staged[place] = product[
                            a * PANEL : (a + 1) * PANEL, b * 2 * PANEL : (b + 1) * 2 * PANEL
                        ]
                        if p <= q:
                            tiles.append((place, p, q))
            return tiles

        ready = []
        for step, (i, j) in enumerate(steps):
            start(ready)
            for deep in range(deeps):
                held = deep % 2
                for unit in range(UNITS):
                    pltpu.matmul_push_rhs(
                        right(j * GROUP + unit * wide, deep), held, unit, transpose=True
                    )
                rows = left(i * GROUP, deep)
                for unit in range(UNITS):
                    pltpu.matmul_acc_lhs(sums[2 * unit + step % 2], rows, load_staged_rhs=held)
            ready = drain(step - 1) if step else []
        start(ready)
        start(drain(len(steps) - 1))

    pl.run_scoped(
        run,
        *[
            pltpu.ACC(unit)((GROUP * PANEL, DEEP), jnp.float32)
            for unit in range(UNITS)
            for _ in range(2)
        ],
    )
    pltpu.make_async_copy(out_ref, out_ref, sem).wait()


def body(voltages, tile_pairs):
    parts, chans, inputs_here, spectra = voltages.shape
    devices = lax.axis_size("chan") * lax.axis_size("tile")
    slots = tile_pairs.shape[0]
    panels = devices * inputs_here // PANEL
    blocks = panels // GROUP

    place = tile_pairs[:, 0] * panels + tile_pairs[:, 1]
    found = place[None, :] == jnp.arange(panels * panels, dtype=jnp.int32)[:, None]
    slot_of = jnp.sum(
        jnp.where(found, jnp.arange(slots, dtype=jnp.int32)[None, :], 0), axis=1
    )

    sent = pl.pallas_call(
        by_channel,
        out_shape=pltpu.VMEM(
            (chans, parts, spectra // LANES, inputs_here, LANES), voltages.dtype
        ),
        in_specs=[pl.BlockSpec(memory_space=pltpu.HBM)],
        out_specs=pl.BlockSpec(memory_space=pltpu.VMEM),
        scratch_shapes=[pltpu.SemaphoreType.DMA],
        compiler_params=pltpu.CompilerParams(vmem_limit_bytes=2**20),
        name="by_channel",
    )(pltpu.with_memory_space_constraint(voltages, pltpu.HBM))
    sent, slot_of = lax.optimization_barrier((sent, slot_of))
    turned = lax.all_to_all(sent, AXES, split_axis=0, concat_axis=0, tiled=True)
    turned = pltpu.with_memory_space_constraint(turned, pltpu.VMEM)
    return pl.pallas_call(
        lambda *refs: visibilities(*refs, panels=panels, scale=spectra**-0.5),
        out_shape=jax.ShapeDtypeStruct((slots, 1, PANEL, 2 * PANEL), jnp.float32),
        in_specs=[
            pl.BlockSpec(memory_space=pltpu.SMEM),
            pl.BlockSpec(memory_space=pltpu.VMEM),
        ],
        out_specs=pl.BlockSpec(memory_space=pl.ANY),
        scratch_shapes=[
            pltpu.VMEM((blocks * (blocks + 1) // 2 * GROUP * GROUP, PANEL, 2 * PANEL), jnp.float32),
            pltpu.SemaphoreType.DMA,
        ],
        compiler_params=pltpu.CompilerParams(vmem_limit_bytes=24 * 2**20),
        cost_estimate=pl.CostEstimate(
            flops=2 * slots * PANEL * 2 * PANEL * 2 * spectra,
            bytes_accessed=slots * PANEL * 2 * PANEL * 4,
            transcendentals=0,
        ),
        name="visibilities",
    )(slot_of, turned)


def solution(mesh):
    placed = (P(None, None, AXES, None), P())
    return jax.shard_map(
        body,
        mesh=mesh,
        in_specs=placed,
        out_specs=P(None, AXES, None, None),
        check_vma=False,
    )
```

```python
import jax
import jax.numpy as jnp
from jax import lax
from jax.experimental import pallas as pl
from jax.experimental.pallas import tpu as pltpu
from jax.sharding import PartitionSpec as P

AXES = ("chan", "tile")
PANEL = 64
LANES = 128
DEEP = 256
UNITS = 2
WIDE = DEEP // (2 * PANEL)
TALL = 2
HELD = 4


def by_channel(x_ref, pairs_ref, y_ref, slot_ref, pairs, sem, pairs_sem, *, panels):
    parts, _, _, spectra = x_ref.shape
    fetch = pltpu.make_async_copy(pairs_ref, pairs, pairs_sem)
    fetch.start()
    for c in range(parts):
        for k in range(spectra // LANES):
            pltpu.make_async_copy(
                x_ref.at[c, :, :, pl.ds(k * LANES, LANES)], y_ref.at[:, c, k], sem
            ).start()
    fetch.wait()
    here = lax.broadcasted_iota(jnp.int32, slot_ref.shape, 0) * LANES
    here = here + lax.broadcasted_iota(jnp.int32, slot_ref.shape, 1)

    def note(s, slots):
        return jnp.where(here == pairs[0, s] * panels + pairs[1, s], s, slots)

    slot_ref[...] = lax.fori_loop(0, pairs.shape[1], note, jnp.zeros_like(here), unroll=16)
    pltpu.make_async_copy(y_ref, y_ref, sem).wait()


def visibilities(slot_ref, x_ref, out_ref, staged, sem, *, panels, scale):
    per_panel = PANEL // x_ref.shape[3]
    deep_per_part = x_ref.shape[2] * LANES // DEEP
    deeps = 2 * deep_per_part

    def samples(first, count, part, deep):
        halves = [
            x_ref[first * per_panel : (first + count) * per_panel, part, deep * DEEP // LANES + h]
            .reshape(count * PANEL, LANES)
            for h in range(DEEP // LANES)
        ]
        return jnp.concatenate(halves, axis=1)

    def left(piece, deep):
        return samples(piece * TALL, TALL, deep // deep_per_part, deep % deep_per_part)

    def right(column, deep):
        part, deep = deep // deep_per_part, deep % deep_per_part
        rows = []
        for q in range(column * WIDE, (column + 1) * WIDE):
            if part == 0:
                rows += [samples(q, 1, 0, deep), -samples(q, 1, 1, deep)]
            else:
                rows += [samples(q, 1, 1, deep), samples(q, 1, 0, deep)]
        return jnp.concatenate(rows, axis=0)

    tasks = [[] for _ in range(UNITS)]
    place_of = {}
    for column in range(panels // WIDE):
        unit = (column + column // UNITS) % UNITS
        pieces = range(((column + 1) * WIDE - 1) // TALL + 1)
        for first in range(0, len(pieces), HELD):
            tasks[unit].append((column, pieces[first : first + HELD]))
        for piece in pieces:
            place_of[column, piece] = len(place_of) * TALL * WIDE

    def run(*sums):
        def total(unit, turn, n):
            return sums[(unit * 2 + turn % 2) * HELD + n]

        def start(tiles):
            for place, p, q in tiles:
                at = p * panels + q
                slot = slot_ref[at // LANES, at % LANES]
                pltpu.make_async_copy(staged.at[place], out_ref.at[slot, 0], sem).start()

        def drain(turn):
            tiles = []
            for unit in range(UNITS):
                if not 0 <= turn < len(tasks[unit]):
                    continue
                column, pieces = tasks[unit][turn]
                for n, piece in enumerate(pieces):
                    product = pltpu.matmul_pop(total(unit, turn, n)) * scale
                    for a in range(TALL):
                        for b in range(WIDE):
                            place = place_of[column, piece] + a * WIDE + b
                            staged[place] = product[
                                a * PANEL : (a + 1) * PANEL, b * 2 * PANEL : (b + 1) * 2 * PANEL
                            ]
                            p, q = piece * TALL + a, column * WIDE + b
                            if p <= q:
                                tiles.append((place, p, q))
            return tiles

        ready = []
        for turn in range(max(map(len, tasks)) + 1):
            start(ready)
            now = [(u, *tasks[u][turn]) for u in range(UNITS) if turn < len(tasks[u])]
            for deep in range(deeps):
                held = deep % 2
                for unit, column, _ in now:
                    pltpu.matmul_push_rhs(right(column, deep), held, unit, transpose=True)
                for n in range(HELD):
                    for unit, _, pieces in now:
                        if n < len(pieces):
                            pltpu.matmul_acc_lhs(
                                total(unit, turn, n),
                                left(pieces[n], deep),
                                load_staged_rhs=None if n else held,
                            )
            ready = drain(turn - 1)
        start(ready)

    pl.run_scoped(
        run,
        *[
            pltpu.ACC(unit)((TALL * PANEL, DEEP), jnp.float32)
            for unit in range(UNITS)
            for _ in range(2 * HELD)
        ],
    )
    pltpu.make_async_copy(out_ref, out_ref, sem).wait()


def body(voltages, tile_pairs):
    parts, chans, inputs_here, spectra = voltages.shape
    devices = lax.axis_size("chan") * lax.axis_size("tile")
    slots = tile_pairs.shape[0]
    panels = devices * inputs_here // PANEL
    tiles = sum(
        (((column + 1) * WIDE - 1) // TALL + 1) * TALL * WIDE for column in range(panels // WIDE)
    )

    sent, slot_of = pl.pallas_call(
        lambda *refs: by_channel(*refs, panels=panels),
        out_shape=(
            pltpu.VMEM((chans, parts, spectra // LANES, inputs_here, LANES), voltages.dtype),
            jax.ShapeDtypeStruct((panels * panels // LANES, LANES), jnp.int32),
        ),
        in_specs=[
            pl.BlockSpec(memory_space=pltpu.HBM),
            pl.BlockSpec(memory_space=pltpu.HBM),
        ],
        out_specs=(
            pl.BlockSpec(memory_space=pltpu.VMEM),
            pl.BlockSpec(memory_space=pltpu.VMEM),
        ),
        scratch_shapes=[
            pltpu.SMEM((2, slots), jnp.int32),
            pltpu.SemaphoreType.DMA,
            pltpu.SemaphoreType.DMA,
        ],
        compiler_params=pltpu.CompilerParams(vmem_limit_bytes=2**20),
        name="by_channel",
    )(
        pltpu.with_memory_space_constraint(voltages, pltpu.HBM),
        pltpu.with_memory_space_constraint(tile_pairs.T, pltpu.HBM),
    )
    turned = lax.all_to_all(sent, AXES, split_axis=0, concat_axis=0, tiled=True)
    turned = pltpu.with_memory_space_constraint(turned, pltpu.VMEM)
    return pl.pallas_call(
        lambda *refs: visibilities(*refs, panels=panels, scale=spectra**-0.5),
        out_shape=jax.ShapeDtypeStruct((slots, 1, PANEL, 2 * PANEL), jnp.float32),
        in_specs=[
            pl.BlockSpec(memory_space=pltpu.SMEM),
            pl.BlockSpec(memory_space=pltpu.VMEM),
        ],
        out_specs=pl.BlockSpec(memory_space=pl.ANY),
        scratch_shapes=[
            pltpu.VMEM((tiles, PANEL, 2 * PANEL), jnp.float32),
            pltpu.SemaphoreType.DMA,
        ],
        compiler_params=pltpu.CompilerParams(vmem_limit_bytes=24 * 2**20),
        cost_estimate=pl.CostEstimate(
            flops=2 * slots * PANEL * 2 * PANEL * 2 * spectra,
            bytes_accessed=slots * PANEL * 2 * PANEL * 4,
            transcendentals=0,
        ),
        name="visibilities",
    )(slot_of, turned)


def solution(mesh):
    placed = (P(None, None, AXES, None), P())
    return jax.shard_map(
        body,
        mesh=mesh,
        in_specs=placed,
        out_specs=P(None, AXES, None, None),
        check_vma=False,
    )
```

```python
import jax
import jax.numpy as jnp
from jax import lax
from jax.experimental import pallas as pl
from jax.experimental.pallas import tpu as pltpu
from jax.sharding import PartitionSpec as P

AXES = ("chan", "tile")
PANEL = 64
LANES = 128
DEEP = 256
UNITS = 2
WIDE = DEEP // (2 * PANEL)
TALL = 2
HELD = 4


def by_channel(x_ref, pairs_ref, y_ref, slot_ref, pairs, sem, pairs_sem, *, panels):
    parts, _, _, spectra = x_ref.shape
    fetch = pltpu.make_async_copy(pairs_ref, pairs, pairs_sem)
    fetch.start()
    for c in range(parts):
        for k in range(spectra // LANES):
            pltpu.make_async_copy(
                x_ref.at[c, :, :, pl.ds(k * LANES, LANES)], y_ref.at[:, c, k], sem
            ).start()
    fetch.wait()
    panel = lax.broadcasted_iota(jnp.int32, (panels, pairs.shape[1]), 0)
    slot = lax.broadcasted_iota(jnp.int32, panel.shape, 1)
    first, second = panel == pairs[0:1], panel == pairs[1:2]

    def spread(value):
        return lax.dot_general(
            jnp.where(first, value, 0).astype(jnp.bfloat16),
            jnp.where(second, 1, 0).astype(jnp.bfloat16),
            (((1,), (1,)), ((), ())),
            preferred_element_type=jnp.float32,
        ).astype(jnp.int32)

    slot_ref[...] = jnp.minimum(
        spread(slot // 16) * 16 + spread(slot % 16), pairs.shape[1] - 1
    )
    pltpu.make_async_copy(y_ref, y_ref, sem).wait()


def visibilities(slots_ref, x_ref, out_ref, slot_of, staged, slot_sem, sem, *, panels, scale):
    per_panel = PANEL // x_ref.shape[3]
    deep_per_part = x_ref.shape[2] * LANES // DEEP
    deeps = 2 * deep_per_part

    def samples(first, count, part, deep):
        halves = [
            x_ref[first * per_panel : (first + count) * per_panel, part, deep * DEEP // LANES + h]
            .reshape(count * PANEL, LANES)
            for h in range(DEEP // LANES)
        ]
        return jnp.concatenate(halves, axis=1)

    def left(piece, deep):
        return samples(piece * TALL, TALL, deep // deep_per_part, deep % deep_per_part)

    def right(column, deep):
        part, deep = deep // deep_per_part, deep % deep_per_part
        rows = []
        for q in range(column * WIDE, (column + 1) * WIDE):
            if part == 0:
                rows += [samples(q, 1, 0, deep), -samples(q, 1, 1, deep)]
            else:
                rows += [samples(q, 1, 1, deep), samples(q, 1, 0, deep)]
        return jnp.concatenate(rows, axis=0)

    tasks = [[] for _ in range(UNITS)]
    place_of = {}
    for column in range(panels // WIDE):
        unit = (column + column // UNITS) % UNITS
        pieces = range(((column + 1) * WIDE - 1) // TALL + 1)
        for first in range(0, len(pieces), HELD):
            tasks[unit].append((column, pieces[first : first + HELD]))
        for piece in pieces:
            place_of[column, piece] = len(place_of) * TALL * WIDE

    def run(*sums):
        def total(unit, turn, n):
            return sums[(unit * 2 + turn % 2) * HELD + n]

        def start(tiles):
            for place, p, q in tiles:
                pltpu.make_async_copy(
                    staged.at[place], out_ref.at[slot_of[p, q], 0], sem
                ).start()

        def drain(turn):
            tiles = []
            for unit in range(UNITS):
                if not 0 <= turn < len(tasks[unit]):
                    continue
                column, pieces = tasks[unit][turn]
                for n, piece in enumerate(pieces):
                    product = pltpu.matmul_pop(total(unit, turn, n)) * scale
                    for a in range(TALL):
                        for b in range(WIDE):
                            place = place_of[column, piece] + a * WIDE + b
                            staged[place] = product[
                                a * PANEL : (a + 1) * PANEL, b * 2 * PANEL : (b + 1) * 2 * PANEL
                            ]
                            p, q = piece * TALL + a, column * WIDE + b
                            if p <= q:
                                tiles.append((place, p, q))
            return tiles

        fetch = pltpu.make_async_copy(slots_ref, slot_of, slot_sem)
        fetch.start()
        ready = []
        for turn in range(max(map(len, tasks)) + 1):
            if turn == 2:
                fetch.wait()
            start(ready)
            now = [(u, *tasks[u][turn]) for u in range(UNITS) if turn < len(tasks[u])]
            for deep in range(deeps):
                held = deep % 2
                for unit, column, _ in now:
                    pltpu.matmul_push_rhs(right(column, deep), held, unit, transpose=True)
                for n in range(HELD):
                    for unit, _, pieces in now:
                        if n < len(pieces):
                            pltpu.matmul_acc_lhs(
                                total(unit, turn, n),
                                left(pieces[n], deep),
                                load_staged_rhs=None if n else held,
                            )
            ready = drain(turn - 1)
        start(ready)

    pl.run_scoped(
        run,
        *[
            pltpu.ACC(unit)((TALL * PANEL, DEEP), jnp.float32)
            for unit in range(UNITS)
            for _ in range(2 * HELD)
        ],
    )
    pltpu.make_async_copy(out_ref, out_ref, sem).wait()


def body(voltages, tile_pairs):
    parts, chans, inputs_here, spectra = voltages.shape
    devices = lax.axis_size("chan") * lax.axis_size("tile")
    slots = tile_pairs.shape[0]
    panels = devices * inputs_here // PANEL
    tiles = sum(
        (((column + 1) * WIDE - 1) // TALL + 1) * TALL * WIDE for column in range(panels // WIDE)
    )

    sent, slots_of = pl.pallas_call(
        lambda *refs: by_channel(*refs, panels=panels),
        out_shape=(
            pltpu.VMEM((chans, parts, spectra // LANES, inputs_here, LANES), voltages.dtype),
            jax.ShapeDtypeStruct((panels, panels), jnp.int32),
        ),
        in_specs=[
            pl.BlockSpec(memory_space=pltpu.HBM),
            pl.BlockSpec(memory_space=pltpu.HBM),
        ],
        out_specs=(
            pl.BlockSpec(memory_space=pltpu.VMEM),
            pl.BlockSpec(memory_space=pltpu.VMEM),
        ),
        scratch_shapes=[
            pltpu.VMEM((2, slots), jnp.int32),
            pltpu.SemaphoreType.DMA,
            pltpu.SemaphoreType.DMA,
        ],
        compiler_params=pltpu.CompilerParams(vmem_limit_bytes=2**20),
        name="by_channel",
    )(
        pltpu.with_memory_space_constraint(voltages, pltpu.HBM),
        pltpu.with_memory_space_constraint(tile_pairs.T, pltpu.HBM),
    )
    turned = lax.all_to_all(sent, AXES, split_axis=0, concat_axis=0, tiled=True)
    turned = pltpu.with_memory_space_constraint(turned, pltpu.VMEM)
    return pl.pallas_call(
        lambda *refs: visibilities(*refs, panels=panels, scale=spectra**-0.5),
        out_shape=jax.ShapeDtypeStruct((slots, 1, PANEL, 2 * PANEL), jnp.float32),
        in_specs=[
            pl.BlockSpec(memory_space=pl.ANY),
            pl.BlockSpec(memory_space=pltpu.VMEM),
        ],
        out_specs=pl.BlockSpec(memory_space=pl.ANY),
        scratch_shapes=[
            pltpu.SMEM((panels, panels), jnp.int32),
            pltpu.VMEM((tiles, PANEL, 2 * PANEL), jnp.float32),
            pltpu.SemaphoreType.DMA,
            pltpu.SemaphoreType.DMA,
        ],
        compiler_params=pltpu.CompilerParams(vmem_limit_bytes=24 * 2**20),
        cost_estimate=pl.CostEstimate(
            flops=2 * slots * PANEL * 2 * PANEL * 2 * spectra,
            bytes_accessed=slots * PANEL * 2 * PANEL * 4,
            transcendentals=0,
        ),
        name="visibilities",
    )(slots_of, turned)


def solution(mesh):
    placed = (P(None, None, AXES, None), P())
    return jax.shard_map(
        body,
        mesh=mesh,
        in_specs=placed,
        out_specs=P(None, AXES, None, None),
        check_vma=False,
    )
```

```python
import jax
import jax.numpy as jnp
import numpy as np
from jax import lax
from jax.experimental import pallas as pl
from jax.experimental.pallas import tpu as pltpu
from jax.sharding import PartitionSpec as P

AXES = ("chan", "tile")
PANEL = 64
LANES = 128
DEEP = 256
UNITS = 2
CORES = 2
WIDE = DEEP // (2 * PANEL)
TALL = 2
HELD = 4


def by_channel(x_ref, pairs_ref, y_ref, slot_ref, pairs, sem, pairs_sem, *, panels):
    parts, spectra = x_ref.shape[0], x_ref.shape[-1]
    fetch = pltpu.make_async_copy(pairs_ref, pairs, pairs_sem)
    fetch.start()
    for c in range(parts):
        for k in range(spectra // LANES):
            for x in range(y_ref.shape[3]):
                for core in range(y_ref.shape[1]):
                    pltpu.make_async_copy(
                        x_ref.at[c, x, :, :, core, :, pl.ds(k * LANES, LANES)],
                        y_ref.at[:, core, :, x, c, k],
                        sem,
                    ).start()
    fetch.wait()
    panel = lax.broadcasted_iota(jnp.int32, (panels, pairs.shape[1]), 0)
    slot = lax.broadcasted_iota(jnp.int32, panel.shape, 1)
    first, second = panel == pairs[0:1], panel == pairs[1:2]

    def spread(value):
        return lax.dot_general(
            jnp.where(first, value, 0).astype(jnp.bfloat16),
            jnp.where(second, 1, 0).astype(jnp.bfloat16),
            (((1,), (1,)), ((), ())),
            preferred_element_type=jnp.float32,
        ).astype(jnp.int32)

    slot_ref[...] = jnp.minimum(
        spread(slot // 16) * 16 + spread(slot % 16), pairs.shape[1] - 1
    )
    pltpu.make_async_copy(y_ref, y_ref, sem).wait()


def visibilities(slots_ref, x_ref, out_ref, slot_of, staged, slot_sem, sem, *, panels, scale):
    ys, cores, zs, _, _, blocks, inputs_here, _ = x_ref.shape
    chips_per_panel = PANEL // (cores * inputs_here)
    deep_per_part = blocks * LANES // DEEP
    deeps = 2 * deep_per_part

    def samples(first, count, part, deep):
        chips = range(first * chips_per_panel, (first + count) * chips_per_panel)
        halves = []
        for k in range(deep * DEEP // LANES, (deep + 1) * DEEP // LANES):
            rows = [
                x_ref[chip // zs % ys, core, chip % zs, chip // zs // ys, part, k]
                for chip in chips
                for core in range(cores)
            ]
            halves.append(jnp.concatenate(rows, axis=0))
        return jnp.concatenate(halves, axis=1)

    def left(piece, deep):
        return samples(piece * TALL, TALL, deep // deep_per_part, deep % deep_per_part)

    def right(column, deep):
        part, deep = deep // deep_per_part, deep % deep_per_part
        rows = []
        for q in range(column * WIDE, (column + 1) * WIDE):
            if part == 0:
                rows += [samples(q, 1, 0, deep), -samples(q, 1, 1, deep)]
            else:
                rows += [samples(q, 1, 1, deep), samples(q, 1, 0, deep)]
        return jnp.concatenate(rows, axis=0)

    tasks = [[] for _ in range(UNITS)]
    place_of = {}
    for column in range(panels // WIDE):
        unit = (column + column // UNITS) % UNITS
        pieces = range(((column + 1) * WIDE - 1) // TALL + 1)
        for first in range(0, len(pieces), HELD):
            tasks[unit].append((column, pieces[first : first + HELD]))
        for piece in pieces:
            place_of[column, piece] = len(place_of) * TALL * WIDE

    def run(*sums):
        def total(unit, turn, n):
            return sums[(unit * 2 + turn % 2) * HELD + n]

        def start(tiles):
            for place, p, q in tiles:
                pltpu.make_async_copy(
                    staged.at[place], out_ref.at[slot_of[p, q], 0], sem
                ).start()

        def drain(turn):
            tiles = []
            for unit in range(UNITS):
                if not 0 <= turn < len(tasks[unit]):
                    continue
                column, pieces = tasks[unit][turn]
                for n, piece in enumerate(pieces):
                    product = pltpu.matmul_pop(total(unit, turn, n)) * scale
                    for a in range(TALL):
                        for b in range(WIDE):
                            place = place_of[column, piece] + a * WIDE + b
                            staged[place] = product[
                                a * PANEL : (a + 1) * PANEL, b * 2 * PANEL : (b + 1) * 2 * PANEL
                            ]
                            p, q = piece * TALL + a, column * WIDE + b
                            if p <= q:
                                tiles.append((place, p, q))
            return tiles

        fetch = pltpu.make_async_copy(slots_ref, slot_of, slot_sem)
        fetch.start()
        ready = []
        for turn in range(max(map(len, tasks)) + 1):
            if turn == 2:
                fetch.wait()
            start(ready)
            now = [(u, *tasks[u][turn]) for u in range(UNITS) if turn < len(tasks[u])]
            for deep in range(deeps):
                held = deep % 2
                for unit, column, _ in now:
                    pltpu.matmul_push_rhs(right(column, deep), held, unit, transpose=True)
                for n in range(HELD):
                    for unit, _, pieces in now:
                        if n < len(pieces):
                            pltpu.matmul_acc_lhs(
                                total(unit, turn, n),
                                left(pieces[n], deep),
                                load_staged_rhs=None if n else held,
                            )
            ready = drain(turn - 1)
        start(ready)

    pl.run_scoped(
        run,
        *[
            pltpu.ACC(unit)((TALL * PANEL, DEEP), jnp.float32)
            for unit in range(UNITS)
            for _ in range(2 * HELD)
        ],
    )
    pltpu.make_async_copy(out_ref, out_ref, sem).wait()


def body(voltages, tile_pairs):
    parts, chans, inputs_here, spectra = voltages.shape
    xs, tiles_of_x = lax.axis_size("chan"), lax.axis_size("tile")
    devices = xs * tiles_of_x
    ys = zs = round((tiles_of_x // CORES) ** 0.5)
    order = np.arange(devices).reshape(xs, ys, zs, CORES).transpose(1, 3, 2, 0).reshape(-1)
    slots = tile_pairs.shape[0]
    panels = devices * inputs_here // PANEL
    tiles = sum(
        (((column + 1) * WIDE - 1) // TALL + 1) * TALL * WIDE for column in range(panels // WIDE)
    )

    sent, slots_of = pl.pallas_call(
        lambda *refs: by_channel(*refs, panels=panels),
        out_shape=(
            pltpu.VMEM(
                (ys, CORES, zs, xs, parts, spectra // LANES, inputs_here, LANES), voltages.dtype
            ),
            jax.ShapeDtypeStruct((panels, panels), jnp.int32),
        ),
        in_specs=[
            pl.BlockSpec(memory_space=pltpu.HBM),
            pl.BlockSpec(memory_space=pltpu.HBM),
        ],
        out_specs=(
            pl.BlockSpec(memory_space=pltpu.VMEM),
            pl.BlockSpec(memory_space=pltpu.VMEM),
        ),
        scratch_shapes=[
            pltpu.VMEM((2, slots), jnp.int32),
            pltpu.SemaphoreType.DMA,
            pltpu.SemaphoreType.DMA,
        ],
        compiler_params=pltpu.CompilerParams(vmem_limit_bytes=2**20),
        name="by_channel",
    )(
        pltpu.with_memory_space_constraint(
            voltages.reshape(parts, xs, ys, zs, CORES, inputs_here, spectra), pltpu.HBM
        ),
        pltpu.with_memory_space_constraint(tile_pairs.T, pltpu.HBM),
    )
    turned = lax.all_to_all(
        sent.reshape(chans, *sent.shape[4:]),
        AXES,
        split_axis=0,
        concat_axis=0,
        axis_index_groups=[order.tolist()],
        tiled=True,
    ).reshape(sent.shape)
    turned = pltpu.with_memory_space_constraint(turned, pltpu.VMEM)
    return pl.pallas_call(
        lambda *refs: visibilities(*refs, panels=panels, scale=spectra**-0.5),
        out_shape=jax.ShapeDtypeStruct((slots, 1, PANEL, 2 * PANEL), jnp.float32),
        in_specs=[
            pl.BlockSpec(memory_space=pl.ANY),
            pl.BlockSpec(memory_space=pltpu.VMEM),
        ],
        out_specs=pl.BlockSpec(memory_space=pl.ANY),
        scratch_shapes=[
            pltpu.SMEM((panels, panels), jnp.int32),
            pltpu.VMEM((tiles, PANEL, 2 * PANEL), jnp.float32),
            pltpu.SemaphoreType.DMA,
            pltpu.SemaphoreType.DMA,
        ],
        compiler_params=pltpu.CompilerParams(vmem_limit_bytes=24 * 2**20),
        cost_estimate=pl.CostEstimate(
            flops=2 * slots * PANEL * 2 * PANEL * 2 * spectra,
            bytes_accessed=slots * PANEL * 2 * PANEL * 4,
            transcendentals=0,
        ),
        name="visibilities",
    )(slots_of, turned)


def solution(mesh):
    placed = (P(None, None, AXES, None), P())
    return jax.shard_map(
        body,
        mesh=mesh,
        in_specs=placed,
        out_specs=P(None, AXES, None, None),
        check_vma=False,
    )
```
